32 devices in a mesh: sa: 4 (over y, x), gx: 2 (over core), gy: 4 (over z).
Axes of the slice: x: 2, y: 2, z: 4, core: 2. Of those that a mesh axis runs over, the one named last changes fastest.
Arguments:
- vectors: float32 [32, 4, 8, 24, 256], P('sa', 'gx', 'gy'), may hold values from -6 to 6
- gauge_links: float32 [4, 8, 72, 256], P('gx', 'gy'), may hold values from -1 to 1, as said below
Outputs:
- filtered_once: float32 [32, 4, 8, 24, 256], P('sa', 'gx', 'gy')
- filtered_twice: float32 [32, 4, 8, 24, 256], P('sa', 'gx', 'gy')
The draws below stay inside these ranges and needn't reach their ends.
Inputs may be any that keep to these rules, and one draw needn't show every extreme that they name: `gauge_links`: for each site and direction the nine complex entries form a special unitary 3 x 3 matrix.
All inputs are finite; a program needn't handle non-finite values.
Results may differ from the reference program's by a relative error of at most 0.0001.
Values sent between devices are 32-bit elements; how exact they have to be, the bound alone decides.
No kernel may reach another device: no remote copies, remote signals or barrier semaphores. Data moves between devices by JAX's collectives and lax.ppermute only.
A program may use at most 64 MiB of HBM per device.

```python
import jax
import jax.numpy as jnp
from jax import lax

LS = 32
NZ = 4
NT = 64
NX = 4
NY = 8


def complex_mul(left_re, left_im, right_re, right_im):
    return (left_re * right_re - left_im * right_im, left_re * right_im + left_im * right_re)


def normalise_row(row_re, row_im):
    factor = lax.rsqrt(jnp.sum(row_re * row_re + row_im * row_im, axis=-1, keepdims=True))
    return (row_re * factor, row_im * factor)


def draw_gauge_links(key, part):
    base_key = jax.random.fold_in(key, 11)
    first_key, second_key = jax.random.split(base_key)
    dims_now = (NX, NY, NZ * NT, 4, 3, 3)
    matrix_re = jax.random.normal(first_key, dims_now, jnp.float32)
    matrix_im = jax.random.normal(second_key, dims_now, jnp.float32)
    first_re, first_im = normalise_row(matrix_re[..., 0, :], matrix_im[..., 0, :])
    second_re = matrix_re[..., 1, :]
    second_im = matrix_im[..., 1, :]
    inner_re = jnp.sum(first_re * second_re + first_im * second_im, axis=-1, keepdims=True)
    inner_im = jnp.sum(first_re * second_im - first_im * second_re, axis=-1, keepdims=True)
    second_re = second_re - (inner_re * first_re - inner_im * first_im)
    second_im = second_im - (inner_re * first_im + inner_im * first_re)
    second_re, second_im = normalise_row(second_re, second_im)
    term_one = complex_mul(jnp.roll(first_re, -1, axis=-1), jnp.roll(first_im, -1, axis=-1), jnp.roll(second_re, -2, axis=-1), jnp.roll(second_im, -2, axis=-1))
    term_two = complex_mul(jnp.roll(first_re, -2, axis=-1), jnp.roll(first_im, -2, axis=-1), jnp.roll(second_re, -1, axis=-1), jnp.roll(second_im, -1, axis=-1))
    third_re = term_one[0] - term_two[0]
    third_im = -(term_one[1] - term_two[1])
    rows_re = jnp.stack([first_re, second_re, third_re], axis=-2)
    rows_im = jnp.stack([first_im, second_im, third_im], axis=-2)
    combined = jnp.stack([rows_re, rows_im], axis=-3)
    combined = jnp.moveaxis(combined, 2, -1)
    return combined.reshape(NX, NY, 72, NZ * NT).astype(jnp.float32)


def levels(rng, shape, cuts, least, largest):
    loudness, own = 1.0, jax.random.fold_in(rng, 6)
    for position, shards_of in cuts:
        draws = jnp.exp(jax.random.uniform(jax.random.fold_in(own, position), (shards_of,), jnp.float32, least / len(cuts), largest / len(cuts)))
        loudness = loudness * jnp.repeat(draws, shape[position] // shards_of).reshape([-1 if axis == position else 1 for axis in range(len(shape))])
    return loudness


def bell_draw(stream_key, dims, scale, bound, cuts=(), kind=jnp.bfloat16):
    entries = jax.random.normal(stream_key, dims, jnp.float32) * scale
    if len(cuts) > 0:
        entries = levels(stream_key, dims, cuts, -0.22, 0.18) * entries
    return jnp.clip(entries, min=-bound, max=bound).astype(kind)


def setup_inputs(seed: int = 0) -> dict:
    streams_of = jax.random.split(jax.random.key(seed), 3)
    return {
        "vectors": bell_draw(streams_of[0], (LS, NX, NY, 24, NZ * NT), 1.0, 6.0, ((0, 4), (1, 2), (2, 4)), jnp.float32),
        "gauge_links": draw_gauge_links(jax.random.fold_in(streams_of[2], 71), 0),
    }


m5_height = 1.8
wall_mass = 0.1
cheb_scale = 0.2
cheb_shift = -0.5
gamma_source = ((3, 2, 1, 0), (3, 2, 1, 0), (2, 3, 0, 1), (2, 3, 0, 1))
gamma_real = ((0, 0, 0, 0), (-1, 1, 1, -1), (0, 0, 0, 0), (1, 1, 1, 1))
gamma_imag = ((-1, -1, 1, 1), (0, 0, 0, 0), (-1, 1, 1, -1), (0, 0, 0, 0))


def split_spin(spinor):
    return spinor.reshape(spinor.shape[:-2] + (4, 2, 3, spinor.shape[-1]))


def join_spin(spinor):
    return spinor.reshape(spinor.shape[:-4] + (24, spinor.shape[-1]))


def gamma_times(spinor, direction, sign):
    pieces = []
    for spin_index in range(4):
        source = spinor[..., gamma_source[direction][spin_index], :, :, :]
        own_spin = spinor[..., spin_index, :, :, :]
        coef_re = sign * gamma_real[direction][spin_index]
        coef_im = sign * gamma_imag[direction][spin_index]
        new_re = own_spin[..., 0, :, :] + coef_re * source[..., 0, :, :] - coef_im * source[..., 1, :, :]
        new_im = own_spin[..., 1, :, :] + coef_re * source[..., 1, :, :] + coef_im * source[..., 0, :, :]
        pieces.append(jnp.stack([new_re, new_im], axis=-3))
    return jnp.stack(pieces, axis=-4)


def colour_times(link_dir, spinor, adjoint):
    link_re = link_dir[:, :, 0]
    link_im = link_dir[:, :, 1]
    if adjoint:
        link_re = jnp.swapaxes(link_re, 2, 3)
        link_im = -jnp.swapaxes(link_im, 2, 3)
    link_re = link_re[None, :, :, None]
    link_im = link_im[None, :, :, None]
    spin_re = spinor[..., 0, :, :][..., None, :, :]
    spin_im = spinor[..., 1, :, :][..., None, :, :]
    out_re = jnp.sum(link_re * spin_re - link_im * spin_im, axis=-2)
    out_im = jnp.sum(link_re * spin_im + link_im * spin_re, axis=-2)
    return jnp.stack([out_re, out_im], axis=-3)


def along_local(spinor, direction, stride):
    local_cells = spinor.shape[-1]
    if direction == 2:
        return jnp.roll(spinor, -stride * NT, axis=-1)
    time_index = jnp.arange(local_cells, dtype=jnp.int32) % NT
    if stride == 1:
        return jnp.where(time_index == NT - 1, -jnp.roll(spinor, NT - 1, axis=-1), jnp.roll(spinor, -1, axis=-1))
    return jnp.where(time_index == 0, -jnp.roll(spinor, 1 - NT, axis=-1), jnp.roll(spinor, 1, axis=-1))


def shift_global(spinor, direction, stride):
    if direction < 2:
        return jnp.roll(spinor, -stride, axis=direction + 1)
    return along_local(spinor, direction, stride)


def hopping(spinor, gauge):
    hop_sum = jnp.zeros_like(spinor)
    for direction in range(4):
        link_dir = gauge[:, :, direction]
        ahead_site = shift_global(spinor, direction, 1)
        forward = colour_times(link_dir, gamma_times(ahead_site, direction, -1), False)
        backward = colour_times(link_dir, gamma_times(spinor, direction, 1), True)
        hop_sum = hop_sum + forward + shift_global(backward, direction, -1)
    return -0.5 * hop_sum


def chiral_hops(spinor):
    slices = jnp.arange(LS, dtype=jnp.int32)[:, None, None, None, None]
    upper_half = jnp.roll(spinor, 1, axis=0)
    upper_half = jnp.where(slices == 0, -wall_mass * upper_half, upper_half)
    lower_half = jnp.roll(spinor, -1, axis=0)
    lower_half = jnp.where(slices == LS - 1, -wall_mass * lower_half, lower_half)
    return jnp.concatenate([upper_half[:, :, :, :12], lower_half[:, :, :, 12:]], axis=3)


def gamma_five(spinor):
    return jnp.concatenate([spinor[:, :, :, :12], -spinor[:, :, :, 12:]], axis=3)


def dirac_operator(spinor, gauge):
    hop_term = join_spin(hopping(split_spin(spinor), gauge))
    return (5.0 - m5_height) * spinor + hop_term - chiral_hops(spinor)


def hermitian(spinor, gauge):
    return gamma_five(dirac_operator(spinor, gauge)[::-1])


def reference(vectors, gauge_links):
    gauge = gauge_links.reshape(gauge_links.shape[:2] + (4, 2, 3, 3, gauge_links.shape[-1]))
    filtered_once = cheb_scale * hermitian(vectors, gauge) + cheb_shift * vectors
    filtered_twice = 2.0 * (cheb_scale * hermitian(filtered_once, gauge) + cheb_shift * filtered_once) - vectors
    return filtered_once, filtered_twice
```

```python
import functools

import jax
import jax.numpy as jnp
from jax import lax
from jax.experimental import pallas as pl
from jax.experimental.pallas import tpu as pltpu
from jax.sharding import PartitionSpec as P

NT = 64
LANES = 128

m5_height = 1.8
wall_mass = 0.1
cheb_scale = 0.2
cheb_shift = -0.5
gamma_source = ((3, 2, 1, 0), (3, 2, 1, 0), (2, 3, 0, 1), (2, 3, 0, 1))
gamma_coef = ((-1j, -1j, 1j, 1j), (-1, 1, 1, -1), (-1j, 1j, 1j, -1j), (1, 1, 1, 1))


def row(spin, part, colour):
    return spin * 6 + part * 3 + colour


def add_times(own, coef, other):
    re, im = other
    if coef == 1:
        term = ((1, re), (1, im))
    elif coef == -1:
        term = ((-1, re), (-1, im))
    elif coef == 1j:
        term = ((-1, im), (1, re))
    else:
        term = ((1, im), (-1, re))
    out = []
    for mine, (sign, value) in zip(own, term):
        if mine is None:
            out.append(value if sign == 1 else -value)
        else:
            out.append(mine + value if sign == 1 else mine - value)
    return tuple(out)


def project(load, mu, sign):
    half = []
    for spin in range(2):
        other = gamma_source[mu][spin]
        coef = -sign * gamma_coef[mu][spin]
        colours = []
        for colour in range(3):
            own = (load(row(spin, 0, colour)), load(row(spin, 1, colour)))
            src = (load(row(other, 0, colour)), load(row(other, 1, colour)))
            colours.append(add_times(own, coef, src))
        half.append(colours)
    return half


def colour_times(link, half, adjoint):
    result = [[None] * 3 for _ in half]
    for out in range(3):
        entries = []
        for inner in range(3):
            a, b = (inner, out) if adjoint else (out, inner)
            entries.append((link(0, a, b), link(1, a, b)))
        for spin, colours in enumerate(half):
            re = im = None
            for (u_re, u_im), (h_re, h_im) in zip(entries, colours):
                cross = u_im * h_im
                if adjoint:
                    part_re = u_re * h_re + cross
                    part_im = u_re * h_im - u_im * h_re
                else:
                    part_re = u_re * h_re - cross
                    part_im = u_re * h_im + u_im * h_re
                re = part_re if re is None else re + part_re
                im = part_im if im is None else im + part_im
            result[spin][out] = (re, im)
    return result


def rebuild(total, half, mu, sign):
    for spin in range(2):
        for colour in range(3):
            total[spin][colour] = add_times(total[spin][colour], 1, half[spin][colour])
    for spin in range(2, 4):
        coef = -sign * gamma_coef[mu][spin]
        for colour in range(3):
            total[spin][colour] = add_times(total[spin][colour], coef, half[gamma_source[mu][spin]][colour])


def empty():
    return [[(None, None)] * 3 for _ in range(4)]


def each(half, step):
    return [[(step(re), step(im)) for re, im in colours] for colours in half]


def lane_index(shape):
    return lax.broadcasted_iota(jnp.int32, shape, len(shape) - 1)


def step_t(value, stride):
    lanes = value.shape[-1]
    t = lane_index(value.shape) % NT
    if stride == 1:
        inner, outer, edge = pltpu.roll(value, lanes - 1, 1), pltpu.roll(value, NT - 1, 1), NT - 1
    else:
        inner, outer, edge = pltpu.roll(value, 1, 1), pltpu.roll(value, lanes - NT + 1, 1), 0
    return jnp.where(t == edge, -outer, inner)


def step_z(values, stride):
    turned = [pltpu.roll(value, NT, 1) for value in values]
    low = lane_index(values[0].shape) < NT
    count = len(values)
    if stride == 1:
        return [jnp.where(low, turned[k], turned[(k + 1) % count]) for k in range(count)]
    return [jnp.where(low, turned[(k - 1) % count], turned[k]) for k in range(count)]


def loader(ref, site, lanes):
    return lambda index: ref[site + (index, slice(None), lanes)]


def link_loader(ref, site, mu, lanes):
    return lambda part, a, b: ref[site + (pl.ds(mu * 18 + part * 9 + a * 3 + b, 1), lanes)]


def store_half(ref, site, half, lanes):
    for spin in range(2):
        for colour in range(3):
            for part in range(2):
                ref[site + (row(spin, part, colour), slice(None), lanes)] = half[spin][colour][part]


def load_half(ref, site, lanes):
    return [
        [tuple(ref[site + (row(spin, part, colour), slice(None), lanes)] for part in range(2)) for colour in range(3)]
        for spin in range(2)
    ]


def lane_blocks(cells):
    return [slice(start, start + LANES) for start in range(0, cells, LANES)]


def to_slices_last(source, slices):
    if slices % 8 == 0:
        return jnp.swapaxes(source, 0, 1)
    return jnp.stack([source[s] for s in range(slices)], axis=1)


def to_slices_first(source, slices):
    if slices % 8 == 0:
        return jnp.swapaxes(source, 0, 1)
    return jnp.stack([source[:, s] for s in range(slices)], axis=0)


def write_faces(field, gauge, site, here, there, up_ref, down_ref, mu, sign, lanes):
    at, extent = here
    if at == extent - 1:
        half = project(loader(field, site, lanes), mu, -sign)
        half = colour_times(link_loader(gauge, site, mu, lanes), half, True)
        store_half(up_ref, there, half, lanes)
    if at == 0:
        store_half(down_ref, there, project(loader(field, site, lanes), mu, sign), lanes)


def local_hops(field, gauge, total_ref, sites, sign):
    extent_x, extent_y = sites
    cells = field.shape[-1]
    blocks = lane_blocks(cells)
    for x in range(extent_x):
        for y in range(extent_y):
            site = (x, y)
            ahead, behind = [], []
            for lanes in blocks:
                load = loader(field, site, lanes)
                ahead.append(project(load, 2, sign))
                behind.append(colour_times(link_loader(gauge, site, 2, lanes), project(load, 2, -sign), True))
            for spin in range(2):
                for colour in range(3):
                    for halves, stride in ((ahead, 1), (behind, -1)):
                        moved = [
                            step_z([half[spin][colour][part] for half in halves], stride) for part in range(2)
                        ]
                        for k in range(len(blocks)):
                            halves[k][spin][colour] = (moved[0][k], moved[1][k])
            for k, lanes in enumerate(blocks):
                load = loader(field, site, lanes)
                total = empty()
                rebuild(total, colour_times(link_loader(gauge, site, 2, lanes), ahead[k], False), 2, sign)
                rebuild(total, behind[k], 2, -sign)
                half = each(project(load, 3, sign), lambda value: step_t(value, 1))
                rebuild(total, colour_times(link_loader(gauge, site, 3, lanes), half, False), 3, sign)
                half = colour_times(link_loader(gauge, site, 3, lanes), project(load, 3, -sign), True)
                rebuild(total, each(half, lambda value: step_t(value, -1)), 3, -sign)
                for mu, at, extent in ((0, x, extent_x), (1, y, extent_y)):
                    move = (1, 0) if mu == 0 else (0, 1)
                    if at + 1 < extent:
                        other = (x + move[0], y + move[1])
                        half = project(loader(field, other, lanes), mu, sign)
                        rebuild(total, colour_times(link_loader(gauge, site, mu, lanes), half, False), mu, sign)
                    if at > 0:
                        other = (x - move[0], y - move[1])
                        half = project(loader(field, other, lanes), mu, -sign)
                        rebuild(total, colour_times(link_loader(gauge, other, mu, lanes), half, True), mu, -sign)
                for spin in range(4):
                    for colour in range(3):
                        for part in range(2):
                            total_ref[site + (row(spin, part, colour), slice(None), lanes)] = total[spin][colour][part]


def with_halos(total_ref, gauge, site, extents, halos, sign, lanes):
    total = [
        [
            tuple(total_ref[site + (row(spin, part, colour), slice(None), lanes)] for part in range(2))
            for colour in range(3)
        ]
        for spin in range(4)
    ]
    for mu in range(2):
        at, extent = site[mu], extents[mu]
        from_behind, from_ahead = halos[mu]
        there = (site[1 - mu],)
        if at == extent - 1:
            half = load_half(from_ahead, there, lanes)
            rebuild(total, colour_times(link_loader(gauge, site, mu, lanes), half, False), mu, sign)
        if at == 0:
            rebuild(total, load_half(from_behind, there, lanes), mu, -sign)
    return total


def fifth_hop(field, site, index, lanes, towards, edge):
    value = field[site + (index, slice(None), lanes)]
    slices = value.shape[0]
    if slices == 1:
        return edge
    at = lax.broadcasted_iota(jnp.int32, value.shape, 0)
    if towards == -1:
        return jnp.where(at == 0, edge, pltpu.roll(value, 1, 0))
    return jnp.where(at == slices - 1, edge, pltpu.roll(value, slices - 1, 0))


def position():
    return lax.axis_index("sa"), lax.axis_size("sa")


def matched(devices):
    return devices == 4


def to_next_scale(place, last):
    return jnp.where(place == last, -wall_mass, 1.0).astype(jnp.float32)


def to_prior_scale(place):
    return jnp.where(place == 0, -wall_mass, 1.0).astype(jnp.float32)


def pick_edges(first, second):
    place, devices = position()
    if not matched(devices):
        return first, second
    odd = place % 2 == 1
    return (
        lambda *at: jnp.where(odd, second(*at), first(*at)),
        lambda *at: jnp.where(odd, first(*at), second(*at)),
    )


def faces_kernel(v, gauge, field, up_y, down_y, up_x, down_x, edge_a, edge_b):
    slices, extent_x, extent_y, rows, cells = v.shape
    place, devices = position()
    for x in range(extent_x):
        for y in range(extent_y):
            field[x, y] = to_slices_last(v[:, x, y], slices)
            for lanes in lane_blocks(cells):
                write_faces(field, gauge, (x, y), (y, extent_y), (x,), up_y, down_y, 1, 1, lanes)
                write_faces(field, gauge, (x, y), (x, extent_x), (y,), up_x, down_x, 0, 1, lanes)
            to_next = to_next_scale(place, devices - 1) * v[slices - 1, x, y, :12]
            to_prior = to_prior_scale(place) * v[0, x, y, 12:]
            if matched(devices):
                odd = place % 2 == 1
                edge_a[x, y] = jnp.where(odd, to_next, to_prior)
                edge_b[x, y] = jnp.where(odd, to_prior, to_next)
            else:
                edge_a[x, y] = to_next
                edge_b[x, y] = to_prior


def local_kernel(sign, field, gauge, total_ref):
    local_hops(field, gauge, total_ref, field.shape[:2], sign)


def first_kernel(
    field, gauge, total_ref, behind_y, ahead_y, behind_x, ahead_x, edge_a, edge_b,
    result, natural, up_y, down_y, up_x, down_x, edge_c, edge_d,
):
    extent_x, extent_y, rows, slices, cells = field.shape
    place, devices = position()
    prior, following = pick_edges(
        lambda x, y, r, lanes: edge_a[x, y, pl.ds(r, 1), lanes], lambda x, y, r, lanes: edge_b[x, y, pl.ds(r, 1), lanes]
    )
    halos = ((behind_x, ahead_x), (behind_y, ahead_y))
    for x in range(extent_x):
        for y in range(extent_y):
            site = (x, y)
            for lanes in lane_blocks(cells):
                total = with_halos(total_ref, gauge, site, (extent_x, extent_y), halos, 1, lanes)
                for spin in range(4):
                    for colour in range(3):
                        for part in range(2):
                            index = row(spin, part, colour)
                            if spin < 2:
                                edge = prior(x, y, index, lanes)
                                hop = fifth_hop(field, site, index, lanes, -1, edge)
                            else:
                                edge = following(x, y, index - 12, lanes)
                                hop = fifth_hop(field, site, index, lanes, 1, edge)
                            own = field[site + (index, slice(None), lanes)]
                            result[site + (index, slice(None), lanes)] = (
                                (5.0 - m5_height) * own - 0.5 * total[spin][colour][part] - hop
                            )
                write_faces(result, gauge, site, (y, extent_y), (x,), up_y, down_y, 1, -1, lanes)
                write_faces(result, gauge, site, (x, extent_x), (y,), up_x, down_x, 0, -1, lanes)
            natural[:, x, y] = to_slices_first(result[x, y], slices)
            to_next = to_next_scale(place, devices - 1) * natural[slices - 1, x, y, 12:]
            to_prior = to_prior_scale(place) * natural[0, x, y, :12]
            if matched(devices):
                edge_d[x, y] = jnp.where(place % 2 == 1, to_prior, to_next)
            else:
                edge_c[x, y] = to_next
                edge_d[x, y] = to_prior


def second_kernel(
    field, gauge, total_ref, behind_y, ahead_y, behind_x, ahead_x, edge_c, edge_d, v,
    out, work,
):
    extent_x, extent_y, rows, slices, cells = field.shape
    place, devices = position()
    if matched(devices):
        odd = place % 2 == 1
        zero = jnp.zeros((1, LANES), jnp.float32)
        prior = lambda x, y, r, lanes: jnp.where(odd, edge_d[x, y, pl.ds(r, 1), lanes], zero)
        following = lambda x, y, r, lanes: jnp.where(odd, zero, edge_d[x, y, pl.ds(r, 1), lanes])
    else:
        prior = lambda x, y, r, lanes: edge_c[x, y, pl.ds(r, 1), lanes]
        following = lambda x, y, r, lanes: edge_d[x, y, pl.ds(r, 1), lanes]
    halos = ((behind_x, ahead_x), (behind_y, ahead_y))
    scale = 2.0 * cheb_scale * cheb_scale
    for x in range(extent_x):
        for y in range(extent_y):
            site = (x, y)
            for lanes in lane_blocks(cells):
                total = with_halos(total_ref, gauge, site, (extent_x, extent_y), halos, -1, lanes)
                for spin in range(4):
                    for colour in range(3):
                        for part in range(2):
                            index = row(spin, part, colour)
                            if spin < 2:
                                edge = following(x, y, index, lanes)
                                hop = fifth_hop(field, site, index, lanes, 1, edge)
                            else:
                                edge = prior(x, y, index - 12, lanes)
                                hop = fifth_hop(field, site, index, lanes, -1, edge)
                            own = field[site + (index, slice(None), lanes)]
                            work[index, :, lanes] = scale * (
                                (5.0 - m5_height) * own - 0.5 * total[spin][colour][part] - hop
                            )
            out[:, x, y] = to_slices_first(work[...], slices) + (2.0 * cheb_shift * cheb_shift - 1.0) * v[:, x, y]


def last_kernel(v, partial, mirrored, once, twice):
    slices, extent_x, extent_y, rows, cells = v.shape
    place, devices = position()
    odd = place % 2 == 1
    at_row = lax.broadcasted_iota(jnp.int32, (rows, cells), 0)
    upper = at_row < 12
    scale = 2.0 * cheb_scale * cheb_scale
    zero = jnp.float32(0.0)
    next_scale = jnp.where(odd, scale * to_next_scale(place, devices - 1), zero)
    prior_scale = jnp.where(odd, zero, scale * to_prior_scale(place))
    for x in range(extent_x):
        for y in range(extent_y):
            for s in range(slices):
                other = mirrored[slices - 1 - s, x, y]
                turned = jnp.where(upper, other, -other)
                once[s, x, y] = cheb_scale * turned + cheb_shift * v[s, x, y]
                result = partial[s, x, y] + 4.0 * cheb_scale * cheb_shift * turned
                if matched(devices):
                    if s == slices - 1:
                        result = result - jnp.where(upper, next_scale * other, zero)
                    if s == 0:
                        result = result - jnp.where(upper, zero, prior_scale * other)
                twice[s, x, y] = result


def call(kernel, inputs, shapes, scratch=(), in_vmem=True):
    inputs = [pltpu.with_memory_space_constraint(value, pltpu.VMEM) for value in inputs]
    spec = pl.BlockSpec(memory_space=pltpu.VMEM)
    if in_vmem:
        out_shape = [pltpu.VMEM(shape, jnp.float32) for shape in shapes]
    else:
        out_shape = [jax.ShapeDtypeStruct(shape, jnp.float32) for shape in shapes]
    return pl.pallas_call(
        kernel,
        out_shape=out_shape,
        in_specs=[spec] * len(inputs),
        out_specs=[spec] * len(shapes),
        scratch_shapes=[pltpu.VMEM(shape, jnp.float32) for shape in scratch],
        compiler_params=pltpu.CompilerParams(vmem_limit_bytes=32 * 1024 * 1024),
    )(*inputs)


def ring(axis, steps):
    count = lax.axis_size(axis)
    return [(source, (source + steps) % count) for source in range(count)]


def per_device(v, gauge):
    slices, extent_x, extent_y, rows, cells = v.shape
    devices = lax.axis_size("sa")
    mirror_pairs = [(source, devices - 1 - source) for source in range(devices)]
    matching = [(source, source ^ 1) for source in range(devices)]
    field_shape = (extent_x, extent_y, rows, slices, cells)
    natural_shape = (slices, extent_x, extent_y, rows, cells)
    face_y = (extent_x, rows // 2, slices, cells)
    face_x = (extent_y, rows // 2, slices, cells)
    edge = (extent_x, extent_y, rows // 2, cells)

    field, up_y, down_y, up_x, down_x, edge_a, edge_b = call(
        faces_kernel, (v, gauge), (field_shape, face_y, face_y, face_x, face_x, edge, edge)
    )
    behind_y = lax.ppermute(up_y, "gy", ring("gy", 1))
    ahead_y = lax.ppermute(down_y, "gy", ring("gy", -1))
    behind_x = lax.ppermute(up_x, "gx", ring("gx", 1))
    ahead_x = lax.ppermute(down_x, "gx", ring("gx", -1))
    if matched(devices):
        edge_a = lax.ppermute(edge_a, "sa", mirror_pairs)
        edge_b = lax.ppermute(edge_b, "sa", matching)
    else:
        edge_a = lax.ppermute(edge_a, "sa", ring("sa", 1))
        edge_b = lax.ppermute(edge_b, "sa", ring("sa", -1))
    (total,) = call(functools.partial(local_kernel, 1), (field, gauge), (field_shape,))

    result, natural, up_y, down_y, up_x, down_x, edge_c, edge_d = call(
        first_kernel,
        (field, gauge, total, behind_y, ahead_y, behind_x, ahead_x, edge_a, edge_b),
        (field_shape, natural_shape, face_y, face_y, face_x, face_x, edge, edge),
    )
    mirrored = lax.ppermute(natural, "sa", mirror_pairs)
    behind_y = lax.ppermute(up_y, "gy", ring("gy", 1))
    ahead_y = lax.ppermute(down_y, "gy", ring("gy", -1))
    behind_x = lax.ppermute(up_x, "gx", ring("gx", 1))
    ahead_x = lax.ppermute(down_x, "gx", ring("gx", -1))
    if matched(devices):
        edge_d = lax.ppermute(edge_d, "sa", matching)
    else:
        edge_c = lax.ppermute(edge_c, "sa", ring("sa", 1))
        edge_d = lax.ppermute(edge_d, "sa", ring("sa", -1))
    (total,) = call(functools.partial(local_kernel, -1), (result, gauge), (field_shape,))
    (partial,) = call(
        second_kernel,
        (result, gauge, total, behind_y, ahead_y, behind_x, ahead_x, edge_c, edge_d, v),
        (natural_shape,),
        scratch=((rows, slices, cells),),
    )
    once, twice = call(last_kernel, (v, partial, mirrored), (natural_shape, natural_shape), in_vmem=False)
    return once, twice


def solution(mesh):
    placed = (P("sa", "gx", "gy", None, None), P("gx", "gy", None, None))
    return jax.shard_map(
        per_device,
        mesh=mesh,
        in_specs=placed,
        out_specs=(P("sa", "gx", "gy", None, None), P("sa", "gx", "gy", None, None)),
        check_vma=False,
    )
```
